128 devices in a mesh: row: 8 (over x, core), col: 16 (over z, y).
Axes of the slice: x: 4, y: 4, z: 4, core: 2. Of those that a mesh axis runs over, the one named last changes fastest.
Arguments:
- bem: float32 [2, 16384, 16384], P(None, 'row', 'col'), may hold values from -0.0625 to 0.0625
- face_disp: float32 [2, 25, 512, 2048], P(None, None, 'col', 'row'), may hold values from -6 to 6
- face_map: float32 [16, 25, 2048], P(None, None, 'row'), may hold values from -1.25 to 1.25
- dof_count: int32 [2048], P('row'), may hold values from 9 to 25, as said below
- elem_target: int32 [2048], replicated, may hold values from 0 to 1023, as said below
- live_count: int32 [8], replicated, may hold values from 0 to 256, as said below
- forward_field: float32 [2, 512, 16384], P(None, None, ('col', 'row')), may hold values from -6 to 6
- power_weight: float32 [512], replicated, may hold values from 0.02 to 0.2
Outputs:
- adjoint_field: float32 [2, 512, 16384], P(None, None, ('col', 'row'))
- gradient: float32 [16384], P(('col', 'row'))
The draws below stay inside these ranges and needn't reach their ends.
Inputs may be any that keep to these rules, and one draw needn't show every extreme that they name: `dof_count`: face nodes of an element of order 2, 3 or 4: 9, 16 or 25. `live_count`: every owner's count is a multiple of 8, the counts sum to 1024, and one owner holds 256. `elem_target`: the live slots name every position 0 to 1023 exactly once; block b = position // 128. The live slots of one owner name each block equally often, at most 32 times, and one owner names every block exactly 32 times. Slots that are not live hold 0.
All inputs are finite; a program needn't handle non-finite values.
Results may differ from the reference program's by a relative error of at most 0.000092.
Values sent between devices are 32-bit elements; how exact they have to be, the bound alone decides.
A program may use at most 320 MiB of HBM per device.

```python
import math
import jax
import jax.numpy as jnp
from jax import lax

NB = 16384
PTS = 16
QD = 25
RHS = 512
EB = 128
ELEM_CAP = 256
ELEM_TOT = 2048
N_ROW = 8


def owner_plan(key):
    middle = EB // N_ROW
    order = jax.random.permutation(jax.random.fold_in(key, 11), N_ROW)
    delta = jax.random.randint(jax.random.fold_in(key, 12), (N_ROW // 2,), 0, middle)
    delta = delta.at[0].set(middle)
    paired = jnp.stack([middle + delta, middle - delta], axis=1).reshape(N_ROW)
    return jnp.zeros((N_ROW,), jnp.int32).at[order].set(paired.astype(jnp.int32))


def draw_live_count(key, part):
    quota = owner_plan(key)
    return (quota * N_ROW).astype(jnp.int32)


def draw_elem_target(key, part):
    quota = owner_plan(key)
    key = jax.random.fold_in(key, 2)
    counts = quota * N_ROW
    owner_keys = jax.random.split(jax.random.fold_in(key, 3), N_ROW)
    shuffled = jax.vmap(lambda k: jax.random.permutation(k, ELEM_CAP))(owner_keys).astype(jnp.int32)
    slot_idx = jnp.broadcast_to(jnp.arange(ELEM_CAP, dtype=jnp.int32)[None, :], (N_ROW, ELEM_CAP))
    living = slot_idx < counts[:, None]
    scores = shuffled + jnp.where(living, 0, ELEM_CAP).astype(jnp.int32)
    sorter = jnp.argsort(scores, axis=1, stable=True)
    ranking = jnp.argsort(sorter, axis=1, stable=True).astype(jnp.int32)
    blocks = ranking % N_ROW
    inner = ranking // N_ROW
    offset = jnp.cumsum(quota) - quota
    raw_pos = jnp.minimum(offset[:, None] + inner, EB - 1)
    block_keys = jax.random.split(jax.random.fold_in(key, 4), N_ROW)
    mixing = jax.vmap(lambda k: jax.random.permutation(k, EB))(block_keys).astype(jnp.int32)
    within = mixing[blocks, raw_pos]
    target = jnp.where(living, blocks * EB + within, 0)
    return target.reshape(-1).astype(jnp.int32)


def draw_dof_count(key, part):
    key = jax.random.fold_in(key, 5)
    picked = jax.random.randint(key, (ELEM_TOT,), 0, 3)
    return ((picked + 3) * (picked + 3)).astype(jnp.int32)


def spiked(entries, key, source, target, parts, factor):
    def block_of(dim):
        return (jnp.arange(entries.shape[dim]) // (entries.shape[dim] // parts)).reshape((-1,) + (1,) * (entries.ndim - 1 - dim))

    near = jax.random.permutation(key, parts)[block_of(target)]
    second = (block_of(target) + parts // 2) % parts
    return jnp.where((block_of(source) == near) | (block_of(source) == second), factor * entries, entries)


def steps_of(stream_key, dims, pieces, low, top_value):
    factor_of, own = 1.0, jax.random.fold_in(stream_key, 6)
    for axis_at, blocks in pieces:
        draws = jnp.exp(jax.random.uniform(jax.random.fold_in(own, axis_at), (blocks,), jnp.float32, low / len(pieces), top_value / len(pieces)))
        factor_of = factor_of * jnp.repeat(draws, dims[axis_at] // blocks).reshape([-1 if axis == axis_at else 1 for axis in range(len(dims))])
    return factor_of


def scatter_about(own_key, extent, deviation, limit, shards=(), kind=jnp.bfloat16):
    entries = jax.random.normal(own_key, extent, jnp.float32) * deviation
    if len(shards) > 0:
        entries = steps_of(own_key, extent, shards, -0.22, 0.18) * entries
    return jnp.clip(entries, min=-limit, max=limit).astype(kind)


def gaussian_with(stream_key, shape, deviation, limit, cuts, heavy, kind=jnp.bfloat16):
    entries = deviation * jax.random.normal(stream_key, shape, jnp.float32)
    if cuts:
        entries = entries * steps_of(stream_key, shape, cuts, -0.22, 0.18)
    return jnp.clip(spiked(entries, jax.random.fold_in(stream_key, 3), *heavy), -limit, limit).astype(kind)


def setup_inputs(seed: int = 0) -> dict:
    key_list = jax.random.split(jax.random.key(seed), 9)
    return {
        "bem": gaussian_with(key_list[0], (2, NB, NB), NB ** -0.5, 0.0625, ((1, 8), (2, 16)), (1, 2, 16, 2.0), jnp.float32),
        "face_disp": scatter_about(key_list[1], (2, QD, RHS, ELEM_TOT), 1.0, 6.0, ((2, 16), (3, 8)), jnp.float32),
        "face_map": scatter_about(key_list[2], (PTS, QD, ELEM_TOT), QD ** -0.5, 1.25, ((2, 8),), jnp.float32),
        "dof_count": draw_dof_count(jax.random.fold_in(key_list[8], 71), 0),
        "elem_target": draw_elem_target(jax.random.fold_in(key_list[8], 71), 0),
        "live_count": draw_live_count(jax.random.fold_in(key_list[8], 71), 0),
        "forward_field": scatter_about(key_list[6], (2, RHS, NB), 1.0, 6.0, ((2, 128),), jnp.float32),
        "power_weight": jnp.clip(jnp.exp(jax.random.uniform(key_list[7], (RHS,), jnp.float32, math.log(0.02), math.log(0.2))), 0.02, 0.2),
    }


HIGHEST = lax.Precision.HIGHEST


def surface_traction(face_map, face_disp, dof_count):
    nodes = face_map.shape[1]
    active = lax.broadcasted_iota(jnp.int32, (nodes, dof_count.shape[0]), 0) < dof_count[None, :]
    masked = face_map * active.astype(face_map.dtype)[None]
    return jnp.einsum("pqe,lqre->lpre", masked, face_disp, precision=HIGHEST)


def reference(bem, face_disp, face_map, dof_count, elem_target, live_count, forward_field, power_weight):
    traction = surface_traction(face_map, face_disp, dof_count)
    slot_idx = jnp.arange(ELEM_TOT, dtype=jnp.int32)
    owner_idx = slot_idx // ELEM_CAP
    living = (slot_idx % ELEM_CAP) < live_count[owner_idx]
    values = traction * living.astype(traction.dtype)[None, None, None, :]
    placed = jnp.zeros((2, PTS, RHS, N_ROW * EB), traction.dtype)
    placed = placed.at[:, :, :, elem_target.astype(jnp.int32)].add(values)
    placed = placed.reshape(2, PTS, RHS, N_ROW, EB)
    adjoint_rhs = jnp.transpose(placed, (0, 2, 3, 1, 4)).reshape(2, RHS, NB)
    real_real = jnp.dot(adjoint_rhs[0], bem[0], precision=HIGHEST)
    imag_imag = jnp.dot(adjoint_rhs[1], bem[1], precision=HIGHEST)
    imag_real = jnp.dot(adjoint_rhs[1], bem[0], precision=HIGHEST)
    real_imag = jnp.dot(adjoint_rhs[0], bem[1], precision=HIGHEST)
    adjoint_field = jnp.stack([real_real - imag_imag, imag_real + real_imag])
    gradient = jnp.sum(power_weight[:, None] * (forward_field[0] * adjoint_field[0] + forward_field[1] * adjoint_field[1]), axis=0)
    return adjoint_field, gradient
```

```python
import functools

import jax
import jax.numpy as jnp
from jax import lax
from jax.experimental import pallas as pl
from jax.experimental.pallas import tpu as pltpu
from jax.sharding import PartitionSpec as P

MESH = pl.DeviceIdType.MESH
F32 = jnp.float32
BF16 = jnp.bfloat16

CHUNKS = 4
START = 8
LAST = START + 4 * CHUNKS
STAGES = {
    3: [(1, 0)],
    4: [(1, 1)],
    5: [(2, 0)],
    6: [(2, 1), (1, 2)],
    7: [(3, 0)],
    9: [(3, 1), (1, 3)],
    10: [(2, 2)],
    11: [(2, 3)],
    13: [(3, 2)],
    15: [(3, 3)],
}


def nt(a, b):
    return lax.dot_general(a, b, (((1,), (1,)), ((), ())), preferred_element_type=F32)


def nn(a, b):
    return jnp.dot(a, b, preferred_element_type=F32)


def halves(value):
    high = value.astype(BF16)
    return high, (value - high.astype(F32)).astype(BF16)


def one_hot(condition):
    return jnp.where(condition, 1.0, 0.0).astype(BF16)


def kernel(
    live_ref, target_ref, dof_ref, weight_ref, bem_ref, disp_ref, map_ref, fwd_ref,
    field_ref, grad_ref,
    disp, fmap, fwd, stage, pick, spread, trac, comp, got, rhs, rhs_hi, rhs_lo, bem_hi, bem_lo,
    mine, theirs, joined, partial, grad,
    in_sem, bem_sem, swap_s, swap_r, ag_s, ag_r, pair_s, pair_r, sum_s, sum_r,
):
    row = lax.axis_index("row")
    col = lax.axis_index("col")
    x, core = row // 2, row % 2
    z, y = col // 4, col % 4

    barrier = pltpu.get_barrier_semaphore()
    for d in range(1, 8):
        pl.semaphore_signal(barrier, inc=1, device_id=((row + d) % 8, col), device_id_type=MESH)
    for d in (1, 3):
        near = ((z + d) % 4) * 4 + y
        pl.semaphore_signal(barrier, inc=1, device_id=(row, near), device_id_type=MESH)
        near = z * 4 + (y + d) % 4
        pl.semaphore_signal(barrier, inc=1, device_id=(row, near), device_id_type=MESH)

    loads = [
        pltpu.make_async_copy(map_ref, fmap, in_sem.at[0]),
        pltpu.make_async_copy(disp_ref, disp, in_sem.at[1]),
        pltpu.make_async_copy(fwd_ref, fwd, in_sem.at[2]),
    ]

    def bem_load(i):
        rows = pl.ds(pl.multiple_of(i * 256, 256), 256)
        return pltpu.make_async_copy(
            bem_ref.at[:, rows, :], stage.at[i % 2], bem_sem.at[i % 2]
        )

    loads[0].start()
    loads[1].start()
    bem_load(0).start()
    bem_load(1).start()
    loads[2].start()

    lane = lax.broadcasted_iota(jnp.int32, (8, 256), 1)
    line = lax.broadcasted_iota(jnp.int32, (8, 256), 0)
    count = jnp.zeros((8, 256), jnp.int32)
    for o in range(8):
        count = jnp.where(line == o, live_ref[o], count)
    live = lane < count
    target = target_ref[...]
    block = target >> 7
    within = target & 127
    members = jnp.concatenate(
        [jnp.where(live & (block == b), 1.0, 0.0) for b in range(8)], axis=0
    )
    before = lax.broadcasted_iota(jnp.int32, (256, 256), 0) < lax.broadcasted_iota(
        jnp.int32, (256, 256), 1
    )
    ranks = members * nn(members.astype(BF16), one_hot(before))
    rank = ranks[0:8]
    for b in range(1, 8):
        rank = rank + ranks[b * 8 : b * 8 + 8]
    place = jnp.where(live, block * 32 + rank.astype(jnp.int32), -1)
    own = jnp.sum(jnp.where(line == row, place, 0), axis=0, keepdims=True)
    tall = lax.broadcasted_iota(jnp.int32, (256, 256), 0)
    pick[...] = one_hot(tall == own)
    wide = lax.broadcasted_iota(jnp.int32, (128, 256), 0)
    here = jnp.where(live & (block == row), place - row * 32 + line * 32, -1)
    total = jnp.zeros((128, 256), F32)
    for o in range(8):
        total = total + nt(
            one_hot(wide == within[o : o + 1]), one_hot(tall == here[o : o + 1])
        )
    spread[...] = total.astype(BF16)
    grad[...] = jnp.zeros_like(grad)

    loads[0].wait()
    node = lax.broadcasted_iota(jnp.int32, (25, 256), 0)
    used = node < dof_ref[...]
    for p in range(16):
        fmap[p] = jnp.where(used, fmap[p], 0.0)
    loads[1].wait()

    pl.semaphore_wait(barrier, 11)

    def swap(j, d):
        to = (row + d) % 8
        return pltpu.make_async_remote_copy(
            comp.at[j, pl.ds(pl.multiple_of(to * 32, 32), 32), :],
            got.at[j, pl.ds(pl.multiple_of(row * 32, 32), 32), :],
            swap_s.at[j, d - 1], swap_r.at[j, d - 1],
            device_id=(to, col), device_id_type=MESH,
        )

    def swap_in(j, d):
        origin = (row + 8 - d) % 8
        return pltpu.make_async_remote_copy(
            comp.at[j, pl.ds(pl.multiple_of(row * 32, 32), 32), :],
            got.at[j, pl.ds(pl.multiple_of(origin * 32, 32), 32), :],
            swap_s.at[j, d - 1], swap_r.at[j, d - 1],
            device_id=((row + d) % 8, col), device_id_type=MESH,
        )

    def tractions(j):
        eight = pl.ds(pl.multiple_of(j * 8, 8), 8)
        for group in range(4):
            sums = [[None] * 4, [None] * 4]
            for q in range(25):
                value = [disp[l, q, eight, :] for l in range(2)]
                for k in range(4):
                    scale = fmap[group * 4 + k, q : q + 1, :]
                    for l in range(2):
                        term = scale * value[l]
                        sums[l][k] = term if q == 0 else sums[l][k] + term
            for l in range(2):
                for k in range(4):
                    at = l * 128 + (group * 4 + k) * 8
                    trac[at : at + 8, :] = sums[l][k]
        high, low = halves(trac[...])
        comp[j] = nt(pick[...], high) + nt(pick[...], low)
        for d in range(1, 8):
            swap(j, d).start()
        rows = pl.ds(pl.multiple_of(row * 32, 32), 32)
        got[j, rows, :] = comp[j, rows, :]

    def slots(f, first, second):
        def sel(v):
            kind, a = v
            return (a // 2, a % 2) if kind == "one" else (slice(None), a)

        fi, se = sel(first), sel(second)
        return fi + se if f == 0 else se + fi

    def part(ref, j, f, first, second, half):
        lanes = slice(None) if half is None else pl.ds(half * 1024, 1024)
        return ref.at[(j,) + slots(f, first, second) + (f, slice(None), lanes)]

    def ring(f):
        return (z, y) if f == 0 else (y, z)

    def away(f, axis, step):
        v1, v2 = ring(f)
        if axis == 0:
            v1 = (v1 + step + 4) % 4
        else:
            v2 = (v2 + step + 4) % 4
        return (row, v1 * 4 + v2) if f == 0 else (row, v2 * 4 + v1)

    def hop(j, f, kind):
        v1, v2 = ring(f)
        step = 1 if kind % 2 == 0 else -1
        back = lambda v, n: (v + 4 - n * step) % 4
        one = lambda v: ("one", v)
        par = ("par", (v1 + 1) % 2)
        far = one((v1 + 2) % 4)
        half = kind % 2
        table = {
            0: (0, (one(v1), one(v2), None), (one(back(v1, 1)), one(v2), None)),
            1: (1, (one(v1), one(v2), None), (one(v1), one(back(v2, 1)), None)),
            2: (0, (one(back(v1, 1)), one(v2), half), (far, one(v2), half)),
            3: (1, (par, one(v2), None), (par, one(back(v2, 1)), None)),
            4: (1, (one(v1), one(back(v2, 1)), half), (one(v1), one((v2 + 2) % 4), half)),
            5: (1, (far, one(v2), None), (far, one(back(v2, 1)), None)),
            6: (1, (par, one(back(v2, 1)), half), (par, one((v2 + 2) % 4), half)),
            7: (1, (far, one(back(v2, 1)), half), (far, one((v2 + 2) % 4), half)),
        }
        axis, out, into = table[kind // 2]
        make = lambda src, dst: pltpu.make_async_remote_copy(
            part(rhs, j, f, *src), part(rhs, j, f, *dst),
            ag_s.at[j, f, kind], ag_r.at[j, f, kind],
            device_id=away(f, axis, step), device_id_type=MESH,
        )
        return lambda: make(out, out), lambda: make(out, into)

    def begin(j, kinds):
        for kind in kinds:
            for f in range(2):
                for s in range(2):
                    hop(j, f, 2 * kind + s)[0]().start()

    def arrive(j, kinds):
        for kind in kinds:
            for f in range(2):
                for s in range(2):
                    hop(j, f, 2 * kind + s)[1]().wait_recv()

    def gather_stage(j, which):
        if which == 1:
            arrive(j, (0,))
            begin(j, (2, 3))
            arrive(j, (1,))
            begin(j, (4,))
        elif which == 2:
            arrive(j, (2,))
            begin(j, (5,))
            arrive(j, (3,))
            begin(j, (6,))
        elif which == 3:
            arrive(j, (5,))
            begin(j, (7,))
        else:
            arrive(j, (4, 6, 7))

    def position(j):
        for d in range(1, 8):
            swap_in(j, d).wait_recv()
        high, low = halves(got[j])
        placed = nn(spread[...], high) + nn(spread[...], low)
        placed = placed.T
        for l in range(2):
            for p in range(16):
                at = l * 128 + p * 8
                rhs[j, z // 2, z % 2, y // 2, y % 2, l, :, p * 128 : p * 128 + 128] = placed[
                    at : at + 8, :
                ]
        begin(j, (0, 1))

    def split_bem(i):
        bem_load(i).wait()

        @pl.loop(0, 16)
        def _(k):
            src = pl.ds(pl.multiple_of(k * 16, 16), 16)
            dst = pl.ds(pl.multiple_of(i * 256 + k * 16, 16), 16)
            for l in range(2):
                high, low = halves(stage[i % 2, l, src, :])
                bem_hi[l, dst, :] = high
                bem_lo[l, dst, :] = low

        @pl.when(i + 2 < 8)
        def _():
            bem_load(i + 2).start()

    def split_rhs(j):
        for c in range(16):
            value = rhs[j, c // 8, (c // 4) % 2, (c // 2) % 2, c % 2].reshape(16, 2048)
            high, low = halves(value)
            rhs_hi[c * 16 : c * 16 + 16, :] = high
            rhs_lo[c * 16 : c * 16 + 16, :] = low

    def pair(j, t):
        return pltpu.make_async_remote_copy(
            theirs.at[j, t], joined.at[j, t], pair_s.at[j, t], pair_r.at[j, t],
            device_id=(x * 2 + 1 - core, col), device_id_type=MESH,
        )

    def share(j, t):
        return pltpu.make_async_remote_copy(
            mine.at[j, t], partial.at[j, t], sum_s.at[j, t], sum_r.at[j, t],
            device_id=(((x + 1 + t) % 4) * 2 + core, col), device_id_type=MESH,
        )

    def multiply(j, t):
        cols = pl.ds(pl.multiple_of(((x + 1 + t) % 4) * 256, 256), 256)
        prod = []
        for l in range(2):
            prod.append(
                (
                    nn(rhs_hi[...], bem_hi[l, :, cols])
                    + nn(rhs_hi[...], bem_lo[l, :, cols])
                    + nn(rhs_lo[...], bem_hi[l, :, cols])
                ).reshape(16, 2, 8, 256)
            )
        both = (prod[0][:, 0] - prod[1][:, 1], prod[0][:, 1] + prod[1][:, 0])
        for l in range(2):
            value = both[l].reshape(128, 256)
            left, right = value[:, :128], value[:, 128:]
            mine[j, t, l] = jnp.where(core == 0, left, right)
            theirs[j, t, l] = jnp.where(core == 0, right, left)
        pair(j, t).start()

    def pass_on(j, t):
        pair(j, t).wait_recv()
        mine[j, t] = mine[j, t] + joined[j, t]

        @pl.when(t < 3)
        def _():
            share(j, t).start()

    def finish(j):
        for t in range(3):
            share(j, t).wait_recv()
        eight = pl.ds(pl.multiple_of(j * 8, 8), 8)
        for l in range(2):
            value = mine[j, 3, l] + partial[j, 0, l] + partial[j, 1, l] + partial[j, 2, l]
            value = value.reshape(16, 8, 128)
            field_ref[l, :, eight, :] = value
            grad[...] += jnp.sum(fwd[l, :, eight, :] * value, axis=0)

    def weigh():
        loads[2].wait()
        weight = jnp.broadcast_to(weight_ref[...], (128, 512)).T.reshape(16, 32, 128)
        for l in range(2):
            fwd[l] = fwd[l] * weight

    @pl.loop(0, LAST)
    def _(s):
        for slot, stages in STAGES.items():
            @pl.when(s == slot)
            def _():
                for which, j in stages:
                    gather_stage(j, which)

        @pl.when(s < CHUNKS)
        def _():
            tractions(s)

        @pl.when((s >= 1) & (s <= CHUNKS))
        def _():
            position(s - 1)

        @pl.when(s < 8)
        def _():
            split_bem(s)

        @pl.when(s == 5)
        def _():
            weigh()

        @pl.when(s >= START)
        def _():
            k = s - START
            j, t = k // 4, k % 4

            @pl.when(t == 0)
            def _():
                gather_stage(j, 4)
                split_rhs(j)

            multiply(j, t)

            @pl.when(k >= 1)
            def _():
                pass_on((k - 1) // 4, (k - 1) % 4)

            @pl.when((t == 2) & (j >= 1))
            def _():
                finish(j - 1)

    pass_on(CHUNKS - 1, 3)
    finish(CHUNKS - 1)
    grad_ref[...] = jnp.sum(grad[...], axis=0, keepdims=True)

    for j in range(CHUNKS):
        for d in range(1, 8):
            swap(j, d).wait_send()
        for f in range(2):
            for kind in range(16):
                hop(j, f, kind)[0]().wait_send()
        for t in range(4):
            pair(j, t).wait_send()
        for t in range(3):
            share(j, t).wait_send()


def on_device(
    bem, face_disp, face_map, dof_count, elem_target, live_count, forward_field, power_weight
):
    vmem = pl.BlockSpec(memory_space=pltpu.VMEM)
    hbm = pl.BlockSpec(memory_space=pl.ANY)
    dma = pltpu.SemaphoreType.DMA
    field, gradient = pl.pallas_call(
        kernel,
        out_shape=(
            jax.ShapeDtypeStruct((2, 16, 32, 128), F32),
            jax.ShapeDtypeStruct((1, 128), F32),
        ),
        in_specs=[pl.BlockSpec(memory_space=pltpu.SMEM), vmem, vmem, vmem, hbm, hbm, hbm, hbm],
        out_specs=(vmem, vmem),
        scratch_shapes=[
            pltpu.VMEM((2, 25, 32, 256), F32),
            pltpu.VMEM((16, 25, 256), F32),
            pltpu.VMEM((2, 16, 32, 128), F32),
            pltpu.VMEM((2, 2, 256, 1024), F32),
            pltpu.VMEM((256, 256), BF16),
            pltpu.VMEM((128, 256), BF16),
            pltpu.VMEM((256, 256), F32),
            pltpu.VMEM((CHUNKS, 256, 256), F32),
            pltpu.VMEM((CHUNKS, 256, 256), F32),
            pltpu.VMEM((CHUNKS, 2, 2, 2, 2, 2, 8, 2048), F32),
            pltpu.VMEM((256, 2048), BF16),
            pltpu.VMEM((256, 2048), BF16),
            pltpu.VMEM((2, 2048, 1024), BF16),
            pltpu.VMEM((2, 2048, 1024), BF16),
            pltpu.VMEM((CHUNKS, 4, 2, 128, 128), F32),
            pltpu.VMEM((CHUNKS, 4, 2, 128, 128), F32),
            pltpu.VMEM((CHUNKS, 4, 2, 128, 128), F32),
            pltpu.VMEM((CHUNKS, 3, 2, 128, 128), F32),
            pltpu.VMEM((8, 128), F32),
            dma((3,)),
            dma((2,)),
            dma((CHUNKS, 7)),
            dma((CHUNKS, 7)),
            dma((CHUNKS, 2, 16)),
            dma((CHUNKS, 2, 16)),
            dma((CHUNKS, 4)),
            dma((CHUNKS, 4)),
            dma((CHUNKS, 3)),
            dma((CHUNKS, 3)),
        ],
        compiler_params=pltpu.CompilerParams(
            collective_id=0, has_side_effects=True, vmem_limit_bytes=60 * 2**20
        ),
        cost_estimate=pl.CostEstimate(
            flops=26 * 10**9, bytes_accessed=20 * 10**6, transcendentals=0
        ),
        name="adjoint",
    )(
        live_count,
        elem_target.reshape(8, 256),
        dof_count.reshape(1, 256),
        power_weight.reshape(1, 512),
        bem,
        face_disp,
        face_map,
        forward_field.reshape(2, 16, 32, 128),
    )
    return field.reshape(2, 512, 128), gradient.reshape(128)


def solution(mesh):
    placed = (
        P(None, "row", "col"),
        P(None, None, "col", "row"),
        P(None, None, "row"),
        P("row"),
        P(),
        P(),
        P(None, None, ("col", "row")),
        P(),
    )
    return jax.shard_map(
        on_device,
        mesh=mesh,
        in_specs=placed,
        out_specs=(P(None, None, ("col", "row")), P(("col", "row"))),
        check_vma=False,
    )
```

```python
import functools

import jax
import jax.numpy as jnp
from jax import lax
from jax.experimental import pallas as pl
from jax.experimental.pallas import tpu as pltpu
from jax.sharding import PartitionSpec as P

MESH = pl.DeviceIdType.MESH
F32 = jnp.float32
BF16 = jnp.bfloat16

CHUNKS = 4
UNITS = ((0, 0, 2048), (1, 0, 2048), (2, 0, 2048), (3, 0, 2048))
GROUPS = ((0, 0, 2048), (1, 0, 2048), (2, 0, 2048), (3, 0, 2048))
OPENING = (
    ("T", 1), ("T", 2), ("X", 1), ("B", 0), ("P", 0), ("V", 0, 0), ("B", 1), ("X", 2), ("P", 1),
    ("V", 0, 1), ("T", 3), ("V", 1, 0), ("X", 3), ("P", 2), ("B", 2), ("B", 3), ("V", 2, 0),
    ("V", 1, 1), ("B", 4), ("P", 3), ("V", 3, 0), ("B", 5), ("B", 6), ("V", 0, 2), ("V", 2, 1),
    ("B", 7), ("V", 4, 0),
)
EVENTS = {
    (0, 1): (("V", 1, 2),),
    (0, 2): (("V", 3, 1),),
    (1, 0): (("V", 2, 2), ("V", 0, 3), ("V", 4, 1),),
    (1, 2): (("V", 3, 2),),
    (1, 3): (("V", 1, 3),),
    (2, 0): (("V", 4, 2),),
    (2, 1): (("V", 2, 3),),
    (2, 3): (("V", 3, 3),),
    (3, 0): (("V", 4, 3),),
}
FORWARD = (2, 4, 6, 7)
SEM = (0, 2, 4, 5, 7, 8, 10, 11)

def nt(a, b):
    return lax.dot_general(a, b, (((1,), (1,)), ((), ())), preferred_element_type=F32)


def nn(a, b):
    return jnp.dot(a, b, preferred_element_type=F32)


def halves(value):
    high = value.astype(BF16)
    return high, (value - high.astype(F32)).astype(BF16)


def one_hot(condition):
    return jnp.where(condition, 1.0, 0.0).astype(BF16)


def kernel(
    live_ref, target_ref, dof_ref, weight_ref, bem_ref, disp_ref, map_ref, fwd_ref,
    field_ref, grad_ref,
    disp, fmap, fwd, stage, pick, spread, trac, comp, got, rhs, rhs_hi, rhs_lo, bem_hi, bem_lo,
    mine, theirs, joined, partial, grad,
    in_sem, bem_sem, swap_s, swap_r, ag_s, ag_r, pair_s, pair_r, sum_s, sum_r,
):
    row = lax.axis_index("row")
    col = lax.axis_index("col")
    x, core = row // 2, row % 2
    z, y = col // 4, col % 4

    barrier = pltpu.get_barrier_semaphore()
    for d in range(1, 8):
        pl.semaphore_signal(barrier, inc=1, device_id=((row + d) % 8, col), device_id_type=MESH)
    for d in (1, 3):
        near = ((z + d) % 4) * 4 + y
        pl.semaphore_signal(barrier, inc=1, device_id=(row, near), device_id_type=MESH)
        near = z * 4 + (y + d) % 4
        pl.semaphore_signal(barrier, inc=1, device_id=(row, near), device_id_type=MESH)

    loads = [
        pltpu.make_async_copy(map_ref, fmap, in_sem.at[0]),
        pltpu.make_async_copy(disp_ref, disp, in_sem.at[1]),
        pltpu.make_async_copy(fwd_ref, fwd, in_sem.at[2]),
    ]

    def bem_load(i):
        rows = pl.ds(pl.multiple_of(i * 256, 256), 256)
        return pltpu.make_async_copy(
            bem_ref.at[:, rows, :], stage.at[i % 2], bem_sem.at[i % 2]
        )

    loads[0].start()
    loads[1].start()
    bem_load(0).start()
    bem_load(1).start()
    loads[2].start()

    lane = lax.broadcasted_iota(jnp.int32, (8, 256), 1)
    line = lax.broadcasted_iota(jnp.int32, (8, 256), 0)
    count = jnp.zeros((8, 256), jnp.int32)
    for o in range(8):
        count = jnp.where(line == o, live_ref[o], count)
    live = lane < count
    target = jnp.concatenate([target_ref[:, o * 256 : o * 256 + 256] for o in range(8)], axis=0)
    block = target >> 7
    within = target & 127
    members = jnp.concatenate(
        [jnp.where(live & (block == b), 1.0, 0.0) for b in range(8)], axis=0
    )
    before = lax.broadcasted_iota(jnp.int32, (256, 256), 0) < lax.broadcasted_iota(
        jnp.int32, (256, 256), 1
    )
    ranks = members * nn(members.astype(BF16), one_hot(before))
    rank = ranks[0:8]
    for b in range(1, 8):
        rank = rank + ranks[b * 8 : b * 8 + 8]
    place = jnp.where(live, block * 32 + rank.astype(jnp.int32), -1)
    own = jnp.sum(jnp.where(line == row, place, 0), axis=0, keepdims=True)
    tall = lax.broadcasted_iota(jnp.int32, (256, 256), 0)
    pick[...] = one_hot(tall == own)
    grad[...] = jnp.zeros_like(grad)

    def build_spread():
        wide = lax.broadcasted_iota(jnp.int32, (128, 256), 0)
        here = jnp.where(live & (block == row), place - row * 32 + line * 32, -1)
        total = jnp.zeros((128, 256), F32)
        for o in range(8):
            total = total + nt(
                one_hot(wide == within[o : o + 1]), one_hot(tall == here[o : o + 1])
            )
        spread[...] = total.astype(BF16)

    def mask_map():
        loads[0].wait()
        node = lax.broadcasted_iota(jnp.int32, (25, 16, 256), 0)
        used = node < dof_ref[...].reshape(1, 1, 256)
        fmap[...] = jnp.where(used, fmap[...], 0.0)
        loads[1].wait()

    def swap(j, d):
        to = (row + d) % 8
        return pltpu.make_async_remote_copy(
            comp.at[j, pl.ds(pl.multiple_of(to * 32, 32), 32), :],
            got.at[j, pl.ds(pl.multiple_of(row * 32, 32), 32), :],
            swap_s.at[j, d - 1], swap_r.at[j, d - 1],
            device_id=(to, col), device_id_type=MESH,
        )

    def swap_in(j, d):
        origin = (row + 8 - d) % 8
        return pltpu.make_async_remote_copy(
            comp.at[j, pl.ds(pl.multiple_of(row * 32, 32), 32), :],
            got.at[j, pl.ds(pl.multiple_of(origin * 32, 32), 32), :],
            swap_s.at[j, d - 1], swap_r.at[j, d - 1],
            device_id=((row + d) % 8, col), device_id_type=MESH,
        )

    def tractions(j):
        eight = pl.ds(j * 8, 8)
        for group in range(4):
            sums = [[None] * 4, [None] * 4]
            for q in range(25):
                value = [disp[l, q, eight, :] for l in range(2)]
                for k in range(4):
                    at = group * 4 + k
                    scale = fmap[q, at : at + 1, :]
                    for l in range(2):
                        term = scale * value[l]
                        sums[l][k] = term if q == 0 else sums[l][k] + term
            for l in range(2):
                for k in range(4):
                    at = l * 128 + (group * 4 + k) * 8
                    trac[at : at + 8, :] = sums[l][k]
        high, low = halves(trac[...])
        comp[j] = nt(pick[...], high) + nt(pick[...], low)

    def exchange(j):
        for d in range(1, 8):
            swap(j, d).start()
        rows = pl.ds(pl.multiple_of(row * 32, 32), 32)
        got[j, rows, :] = comp[j, rows, :]

    def slots(f, first, second):
        def sel(v):
            kind, a = v
            return (a // 2, a % 2) if kind == "one" else (slice(None), a)

        fi, se = sel(first), sel(second)
        return fi + se if f == 0 else se + fi

    def part(ref, u, f, first, second):
        j, lane0, size = UNITS[u]
        return ref.at[(j,) + slots(f, first, second) + (f, slice(None), pl.ds(lane0, size))]

    def ring(f):
        return (z, y) if f == 0 else (y, z)

    def away(f, axis, step):
        v1, v2 = ring(f)
        if axis == 0:
            v1 = (v1 + step + 4) % 4
        else:
            v2 = (v2 + step + 4) % 4
        return (row, v1 * 4 + v2) if f == 0 else (row, v2 * 4 + v1)

    turn = 1 - 2 * core

    def hop(u, f, kind, step):
        v1, v2 = ring(f)
        back = lambda v, n: (v + 4 - n * step) % 4
        one = lambda v: ("one", v)
        par = ("par", (v1 + 1) % 2)
        far = one((v1 + 2) % 4)
        axis, out, into = {
            0: (0, (one(v1), one(v2)), (one(back(v1, 1)), one(v2))),
            1: (1, (one(v1), one(v2)), (one(v1), one(back(v2, 1)))),
            2: (0, (one(back(v1, 1)), one(v2)), (far, one(v2))),
            3: (1, (par, one(v2)), (par, one(back(v2, 1)))),
            4: (1, (one(v1), one(back(v2, 1))), (one(v1), one((v2 + 2) % 4))),
            5: (1, (far, one(v2)), (far, one(back(v2, 1)))),
            6: (1, (par, one(back(v2, 1))), (par, one((v2 + 2) % 4))),
            7: (1, (far, one(back(v2, 1))), (far, one((v2 + 2) % 4))),
        }[kind]
        n = SEM[kind] + (0 if kind in FORWARD or step == 1 else 1)
        make = lambda src, dst: pltpu.make_async_remote_copy(
            part(rhs, u, f, *src), part(rhs, u, f, *dst),
            ag_s.at[u, f, n], ag_r.at[u, f, n],
            device_id=away(f, axis, step), device_id_type=MESH,
        )
        return lambda: make(out, out), lambda: make(out, into)

    def steps(kind):
        return (turn,) if kind in FORWARD else (1, -1)

    def begin(u, kinds):
        for kind in kinds:
            for f in range(2):
                for step in steps(kind):
                    hop(u, f, kind, step)[0]().start()

    def arrive(u, kinds):
        for kind in kinds:
            for f in range(2):
                for step in steps(kind):
                    hop(u, f, kind, step)[1]().wait_recv()

    def gather_stage(u, which):
        if which == 0:
            begin(u, (0, 1))
        elif which == 1:
            arrive(u, (0,))
            begin(u, (2, 3))
            arrive(u, (1,))
            begin(u, (4,))
        elif which == 2:
            arrive(u, (2,))
            begin(u, (5,))
            arrive(u, (3,))
            begin(u, (6,))
        elif which == 3:
            arrive(u, (5,))
            begin(u, (7,))
        else:
            arrive(u, (4, 6, 7))

    def position(j):
        for d in range(1, 8):
            swap_in(j, d).wait_recv()
        high, low = halves(got[j])
        placed = nn(spread[...], high) + nn(spread[...], low)
        placed = placed.T
        for l in range(2):
            for p in range(16):
                at = l * 128 + p * 8
                rhs[j, z // 2, z % 2, y // 2, y % 2, l, :, p * 128 : p * 128 + 128] = placed[
                    at : at + 8, :
                ]

    def split_bem(i):
        bem_load(i).wait()

        @pl.loop(0, 16)
        def _(k):
            src = pl.ds(pl.multiple_of(k * 16, 16), 16)
            dst = pl.ds(pl.multiple_of(i * 256 + k * 16, 16), 16)
            real, imag = stage[i % 2, 0, src, :], stage[i % 2, 1, src, :]
            for m, value in enumerate((real, imag - real, real + imag)):
                high, low = halves(value)
                bem_hi[m, dst, :] = high
                bem_lo[m, dst, :] = low

        if i + 2 < 8:
            bem_load(i + 2).start()

    def split_rhs(j, lane0, size):
        lanes = pl.ds(lane0, size)
        for c in range(0, 16, 2):
            at = (j, c // 8, (c // 4) % 2, (c // 2) % 2)
            real = rhs[at + (slice(None), 0, slice(None), lanes)].reshape(16, size)
            imag = rhs[at + (slice(None), 1, slice(None), lanes)].reshape(16, size)
            for m, value in enumerate((real + imag, real, imag)):
                high, low = halves(value)
                rhs_hi[m, c * 8 : c * 8 + 16, lanes] = high
                rhs_lo[m, c * 8 : c * 8 + 16, lanes] = low

    def pair(j, t):
        return pltpu.make_async_remote_copy(
            theirs.at[j, t], joined.at[j, t], pair_s.at[j, t], pair_r.at[j, t],
            device_id=(x * 2 + 1 - core, col), device_id_type=MESH,
        )

    def share(j, t):
        return pltpu.make_async_remote_copy(
            mine.at[j, t], partial.at[j, t], sum_s.at[j, t], sum_r.at[j, t],
            device_id=(((x + 1 + t) % 4) * 2 + core, col), device_id_type=MESH,
        )

    def multiply(j, lane0, size, t):
        cols = pl.ds(pl.multiple_of(((x + 1 + t) % 4) * 256, 256), 256)
        part = pl.ds(lane0, size)
        both, cross, twin = [
            nn(rhs_hi[m, :, part], bem_hi[m, part, cols])
            + nn(rhs_hi[m, :, part], bem_lo[m, part, cols])
            + nn(rhs_lo[m, :, part], bem_hi[m, part, cols])
            for m in range(3)
        ]
        for l, value in enumerate((both - twin, both + cross)):
            left, right = value[:, :128], value[:, 128:]
            first = jnp.where(core == 0, left, right)
            second = jnp.where(core == 0, right, left)
            if lane0 > 0:
                first = mine[j, t, l] + first
                second = theirs[j, t, l] + second
            mine[j, t, l] = first
            theirs[j, t, l] = second
        if lane0 + size == 2048:
            pair(j, t).start()

    def share_if(j, t):
        if isinstance(t, int):
            if t < 3:
                share(j, t).start()
        else:

            @pl.when(t < 3)
            def _():
                share(j, t).start()

    def pass_on(j, t):
        pair(j, t).wait_recv()
        mine[j, t] = mine[j, t] + joined[j, t]

        share_if(j, t)

    def finish(j):
        for t in range(3):
            share(j, t).wait_recv()
        eight = pl.ds(j * 8, 8)
        for l in range(2):
            value = mine[j, 3, l] + partial[j, 0, l] + partial[j, 1, l] + partial[j, 2, l]
            value = value.reshape(16, 8, 128)
            field_ref[l, :, eight, :] = value
            grad[...] += jnp.sum(fwd[l, :, eight, :] * value, axis=0)

    def weigh():
        loads[2].wait()
        weight = jnp.broadcast_to(weight_ref[...], (128, 512)).T.reshape(16, 32, 128)
        for l in range(2):
            fwd[l] = fwd[l] * weight

    def act(op):
        what = op[0]
        if what == "V":
            gather_stage(op[2], op[1])
        elif what == "T":
            tractions(op[1])
        elif what == "X":
            exchange(op[1])
        elif what == "P":
            position(op[1])
        else:
            split_bem(op[1])

    mask_map()
    tractions(0)
    pl.semaphore_wait(barrier, 11)
    exchange(0)
    build_spread()
    for op in OPENING:
        act(op)
    weigh()

    before = None
    for g, (j, lane0, size) in enumerate(GROUPS):
        last = lane0 + size == 2048
        for op in EVENTS.get((g, 0), ()):
            act(op)
        split_rhs(j, lane0, size)

        @pl.loop(0, 4)
        def _(t):
            for k in (1, 2, 3):
                if (g, k) in EVENTS:

                    @pl.when(t == k)
                    def _():
                        for op in EVENTS[(g, k)]:
                            act(op)

            multiply(j, lane0, size, t)
            if last:

                @pl.when(t >= 1)
                def _():
                    pass_on(j, t - 1)

            if before is not None:

                @pl.when(t == 0)
                def _():
                    pass_on(before, 3)

                @pl.when(t == 2)
                def _():
                    finish(before)

        before = j if last else None

    pass_on(CHUNKS - 1, 3)
    finish(CHUNKS - 1)
    grad_ref[...] = jnp.sum(grad[...], axis=0, keepdims=True)

    for u in range(len(UNITS)):
        for f in range(2):
            for kind in range(8):
                for step in steps(kind):
                    hop(u, f, kind, step)[0]().wait_send()
    for j in range(CHUNKS):
        for d in range(1, 8):
            swap(j, d).wait_send()
        for t in range(4):
            pair(j, t).wait_send()
        for t in range(3):
            share(j, t).wait_send()


def on_device(
    bem, face_disp, face_map, dof_count, elem_target, live_count, forward_field, power_weight
):
    vmem = pl.BlockSpec(memory_space=pltpu.VMEM)
    hbm = pl.BlockSpec(memory_space=pl.ANY)
    dma = pltpu.SemaphoreType.DMA
    field, gradient = pl.pallas_call(
        kernel,
        out_shape=(
            jax.ShapeDtypeStruct((2, 16, 32, 128), F32),
            jax.ShapeDtypeStruct((1, 128), F32),
        ),
        in_specs=[pl.BlockSpec(memory_space=pltpu.SMEM), vmem, vmem, vmem, hbm, hbm, hbm, hbm],
        out_specs=(vmem, vmem),
        scratch_shapes=[
            pltpu.VMEM((2, 25, 32, 256), F32),
            pltpu.VMEM((25, 16, 256), F32),
            pltpu.VMEM((2, 16, 32, 128), F32),
            pltpu.VMEM((2, 2, 256, 1024), F32),
            pltpu.VMEM((256, 256), BF16),
            pltpu.VMEM((128, 256), BF16),
            pltpu.VMEM((256, 256), F32),
            pltpu.VMEM((CHUNKS, 256, 256), F32),
            pltpu.VMEM((CHUNKS, 256, 256), F32),
            pltpu.VMEM((CHUNKS, 2, 2, 2, 2, 2, 8, 2048), F32),
            pltpu.VMEM((3, 128, 2048), BF16),
            pltpu.VMEM((3, 128, 2048), BF16),
            pltpu.VMEM((3, 2048, 1024), BF16),
            pltpu.VMEM((3, 2048, 1024), BF16),
            pltpu.VMEM((CHUNKS, 4, 2, 128, 128), F32),
            pltpu.VMEM((CHUNKS, 4, 2, 128, 128), F32),
            pltpu.VMEM((CHUNKS, 4, 2, 128, 128), F32),
            pltpu.VMEM((CHUNKS, 3, 2, 128, 128), F32),
            pltpu.VMEM((8, 128), F32),
            dma((3,)),
            dma((2,)),
            dma((CHUNKS, 7)),
            dma((CHUNKS, 7)),
            dma((len(UNITS), 2, 12)),
            dma((len(UNITS), 2, 12)),
            dma((CHUNKS, 4)),
            dma((CHUNKS, 4)),
            dma((CHUNKS, 3)),
            dma((CHUNKS, 3)),
        ],
        compiler_params=pltpu.CompilerParams(
            collective_id=0, has_side_effects=True, vmem_limit_bytes=60 * 2**20
        ),
        cost_estimate=pl.CostEstimate(
            flops=26 * 10**9, bytes_accessed=20 * 10**6, transcendentals=0
        ),
        name="adjoint",
    )(
        live_count,
        elem_target.reshape(1, 2048),
        dof_count.reshape(1, 256),
        power_weight.reshape(1, 512),
        bem,
        face_disp,
        jnp.transpose(face_map, (1, 0, 2)),
        forward_field.reshape(2, 16, 32, 128),
    )
    return field.reshape(2, 512, 128), gradient.reshape(128)


def solution(mesh):
    placed = (
        P(None, "row", "col"),
        P(None, None, "col", "row"),
        P(None, None, "row"),
        P("row"),
        P(),
        P(),
        P(None, None, ("col", "row")),
        P(),
    )
    return jax.shard_map(
        on_device,
        mesh=mesh,
        in_specs=placed,
        out_specs=(P(None, None, ("col", "row")), P(("col", "row"))),
        check_vma=False,
    )
```

```python
import functools

import jax
import jax.numpy as jnp
from jax import lax
from jax.experimental import pallas as pl
from jax.experimental.pallas import tpu as pltpu
from jax.sharding import PartitionSpec as P

MESH = pl.DeviceIdType.MESH
F32 = jnp.float32
BF16 = jnp.bfloat16

CHUNKS = 4
UNITS = tuple((j, 0, 2048) for j in range(CHUNKS))
GROUPS = ((0, 0, 4), (1, 0, 4), (2, 0, 3), (3, 0, 4), (2, 3, 4))
OPENING = (
    ("B", 0), ("B", 1), ("T", 1), ("X", 1), ("B", 2), ("P", 0), ("V", 0, 0), ("B", 3), ("P", 1),
    ("V", 0, 1), ("T", 2), ("V", 1, 0), ("T", 3), ("X", 2), ("X", 3), ("V", 2, 0), ("B", 4),
    ("V", 1, 1), ("P", 2), ("V", 3, 0), ("P", 3), ("B", 5), ("B", 6), ("V", 0, 2), ("B", 7),
    ("V", 4, 0), ("V", 2, 1),
)
EVENTS = {
    (0, 1): (
        ("V", 1, 2),
    ),
    (0, 2): (
        ("V", 3, 1), ("R", 0, 0),
    ),
    (0, 3): (
        ("V", 0, 3),
    ),
    (1, 0): (
        ("V", 2, 2), ("V", 4, 1),
    ),
    (1, 1): (
        ("V", 1, 3),
    ),
    (1, 3): (
        ("V", 3, 2), ("R", 1, 1), ("F", 0),
    ),
    (2, 0): (
        ("V", 2, 3), ("V", 4, 2),
    ),
    (2, 2): (
        ("V", 3, 3), ("R", 2, 0),
    ),
    (3, 0): (
        ("V", 4, 3),
    ),
    (3, 3): (
        ("R", 3, 2),
    ),
}
AFTER = {
    (0, 2): (
        ("R", 0, 1),
    ),
    (0, 3): (
        ("R", 0, 2),
    ),
    (1, 0): (
        ("R", 0, 3),
    ),
    (1, 1): (
        ("R", 1, 0),
    ),
    (1, 3): (
        ("R", 1, 2),
    ),
    (2, 0): (
        ("R", 1, 3),
    ),
    (2, 2): (
        ("R", 2, 1), ("F", 1),
    ),
    (3, 0): (
        ("R", 2, 2),
    ),
    (3, 1): (
        ("R", 3, 0),
    ),
    (3, 2): (
        ("R", 3, 1),
    ),
    (4, 3): (
        ("R", 3, 3), ("R", 2, 3), ("F", 2), ("F", 3),
    ),
}
FORWARD = (2, 4, 6, 7)
SEM = (0, 2, 4, 5, 7, 8, 10, 11)

def nt(a, b):
    return lax.dot_general(a, b, (((1,), (1,)), ((), ())), preferred_element_type=F32)


def nn(a, b):
    return jnp.dot(a, b, preferred_element_type=F32)


def halves(value):
    high = value.astype(BF16)
    return high, (value - high.astype(F32)).astype(BF16)


def one_hot(condition):
    return jnp.where(condition, 1.0, 0.0).astype(BF16)


def kernel(
    live_ref, target_ref, dof_ref, weight_ref, bem_ref, disp_ref, map_ref, fwd_ref,
    field_ref, grad_ref,
    disp, fmap, fwd, stage, pick, spread, trac, comp, got, rhs, rhs_hi, rhs_lo, bem_hi, bem_lo,
    mine, theirs, joined, partial, grad,
    in_sem, bem_sem, swap_s, swap_r, ag_s, ag_r, pair_s, pair_r, sum_s, sum_r,
):
    row = lax.axis_index("row")
    col = lax.axis_index("col")
    x, core = row // 2, row % 2
    z, y = col // 4, col % 4

    barrier = pltpu.get_barrier_semaphore()
    for d in range(1, 8):
        pl.semaphore_signal(barrier, inc=1, device_id=((row + d) % 8, col), device_id_type=MESH)
    for d in (1, 3):
        near = ((z + d) % 4) * 4 + y
        pl.semaphore_signal(barrier, inc=1, device_id=(row, near), device_id_type=MESH)
        near = z * 4 + (y + d) % 4
        pl.semaphore_signal(barrier, inc=1, device_id=(row, near), device_id_type=MESH)

    loads = [
        pltpu.make_async_copy(map_ref, fmap, in_sem.at[0]),
        pltpu.make_async_copy(disp_ref, disp, in_sem.at[1]),
        pltpu.make_async_copy(fwd_ref, fwd, in_sem.at[2]),
    ]

    def bem_load(i):
        rows = pl.ds(pl.multiple_of(i * 256, 256), 256)
        return pltpu.make_async_copy(
            bem_ref.at[:, rows, :], stage.at[i % 2], bem_sem.at[i % 2]
        )

    loads[0].start()
    loads[1].start()
    bem_load(0).start()
    bem_load(1).start()
    loads[2].start()

    lane = lax.broadcasted_iota(jnp.int32, (8, 256), 1)
    line = lax.broadcasted_iota(jnp.int32, (8, 256), 0)
    count = jnp.zeros((8, 256), jnp.int32)
    for o in range(8):
        count = jnp.where(line == o, live_ref[o], count)
    live = lane < count
    target = jnp.concatenate([target_ref[:, o * 256 : o * 256 + 256] for o in range(8)], axis=0)
    block = target >> 7
    within = target & 127
    members = jnp.concatenate(
        [jnp.where(live & (block == b), 1.0, 0.0) for b in range(8)], axis=0
    )
    before = lax.broadcasted_iota(jnp.int32, (256, 256), 0) < lax.broadcasted_iota(
        jnp.int32, (256, 256), 1
    )
    ranks = members * nn(members.astype(BF16), one_hot(before))
    rank = ranks[0:8]
    for b in range(1, 8):
        rank = rank + ranks[b * 8 : b * 8 + 8]
    place = jnp.where(live, block * 32 + rank.astype(jnp.int32), -1)
    own = jnp.sum(jnp.where(line == row, place, 0), axis=0, keepdims=True)
    tall = lax.broadcasted_iota(jnp.int32, (256, 256), 0)
    pick[...] = one_hot(tall == own)
    grad[...] = jnp.zeros_like(grad)

    def build_spread():
        wide = lax.broadcasted_iota(jnp.int32, (128, 256), 0)
        here = jnp.where(live & (block == row), place - row * 32 + line * 32, -1)
        total = jnp.zeros((128, 256), F32)
        for o in range(8):
            total = total + nt(
                one_hot(wide == within[o : o + 1]), one_hot(tall == here[o : o + 1])
            )
        spread[...] = total.astype(BF16)

    def mask_map():
        loads[0].wait()
        node = lax.broadcasted_iota(jnp.int32, (25, 16, 256), 0)
        used = node < dof_ref[...].reshape(1, 1, 256)
        fmap[...] = jnp.where(used, fmap[...], 0.0)
        loads[1].wait()

    def swap(j, d):
        to = (row + d) % 8
        return pltpu.make_async_remote_copy(
            comp.at[j, pl.ds(pl.multiple_of(to * 32, 32), 32), :],
            got.at[j, pl.ds(pl.multiple_of(row * 32, 32), 32), :],
            swap_s.at[j, d - 1], swap_r.at[j, d - 1],
            device_id=(to, col), device_id_type=MESH,
        )

    def swap_in(j, d):
        origin = (row + 8 - d) % 8
        return pltpu.make_async_remote_copy(
            comp.at[j, pl.ds(pl.multiple_of(row * 32, 32), 32), :],
            got.at[j, pl.ds(pl.multiple_of(origin * 32, 32), 32), :],
            swap_s.at[j, d - 1], swap_r.at[j, d - 1],
            device_id=((row + d) % 8, col), device_id_type=MESH,
        )

    def tractions(j):
        eight = pl.ds(j * 8, 8)
        for group in range(4):
            sums = [[None] * 4, [None] * 4]
            for q in range(25):
                value = [disp[l, q, eight, :] for l in range(2)]
                for k in range(4):
                    at = group * 4 + k
                    scale = fmap[q, at : at + 1, :]
                    for l in range(2):
                        term = scale * value[l]
                        sums[l][k] = term if q == 0 else sums[l][k] + term
            for l in range(2):
                for k in range(4):
                    at = l * 128 + (group * 4 + k) * 8
                    trac[at : at + 8, :] = sums[l][k]
        high, low = halves(trac[...])
        comp[j] = nt(pick[...], high) + nt(pick[...], low)

    def exchange(j):
        for d in (4, 5, 2, 3, 6, 7, 1):
            swap(j, d).start()
        rows = pl.ds(pl.multiple_of(row * 32, 32), 32)
        got[j, rows, :] = comp[j, rows, :]

    def slots(f, first, second):
        def sel(v):
            kind, a = v
            return (a // 2, a % 2) if kind == "one" else (slice(None), a)

        fi, se = sel(first), sel(second)
        return fi + se if f == 0 else se + fi

    def part(ref, u, f, first, second):
        j, lane0, size = UNITS[u]
        return ref.at[(j,) + slots(f, first, second) + (f, slice(None), pl.ds(lane0, size))]

    def ring(f):
        return (z, y) if f == 0 else (y, z)

    def away(f, axis, step):
        v1, v2 = ring(f)
        if axis == 0:
            v1 = (v1 + step + 4) % 4
        else:
            v2 = (v2 + step + 4) % 4
        return (row, v1 * 4 + v2) if f == 0 else (row, v2 * 4 + v1)

    turn = 1 - 2 * core

    def hop(u, f, kind, step):
        v1, v2 = ring(f)
        back = lambda v, n: (v + 4 - n * step) % 4
        one = lambda v: ("one", v)
        par = ("par", (v1 + 1) % 2)
        far = one((v1 + 2) % 4)
        axis, out, into = {
            0: (0, (one(v1), one(v2)), (one(back(v1, 1)), one(v2))),
            1: (1, (one(v1), one(v2)), (one(v1), one(back(v2, 1)))),
            2: (0, (one(back(v1, 1)), one(v2)), (far, one(v2))),
            3: (1, (par, one(v2)), (par, one(back(v2, 1)))),
            4: (1, (one(v1), one(back(v2, 1))), (one(v1), one((v2 + 2) % 4))),
            5: (1, (far, one(v2)), (far, one(back(v2, 1)))),
            6: (1, (par, one(back(v2, 1))), (par, one((v2 + 2) % 4))),
            7: (1, (far, one(back(v2, 1))), (far, one((v2 + 2) % 4))),
        }[kind]
        n = SEM[kind] + (0 if kind in FORWARD or step == 1 else 1)
        make = lambda src, dst: pltpu.make_async_remote_copy(
            part(rhs, u, f, *src), part(rhs, u, f, *dst),
            ag_s.at[u, f, n], ag_r.at[u, f, n],
            device_id=away(f, axis, step), device_id_type=MESH,
        )
        return lambda: make(out, out), lambda: make(out, into)

    def steps(kind):
        return (turn,) if kind in FORWARD else (1, -1)

    def begin(u, kinds):
        for kind in kinds:
            for f in range(2):
                for step in steps(kind):
                    hop(u, f, kind, step)[0]().start()

    def arrive(u, kinds):
        for kind in kinds:
            for f in range(2):
                for step in steps(kind):
                    hop(u, f, kind, step)[1]().wait_recv()

    def gather_stage(u, which):
        if which == 0:
            begin(u, (0, 1))
        elif which == 1:
            arrive(u, (0,))
            begin(u, (2, 3))
            arrive(u, (1,))
            begin(u, (4,))
        elif which == 2:
            arrive(u, (2,))
            begin(u, (5,))
            arrive(u, (3,))
            begin(u, (6,))
        elif which == 3:
            arrive(u, (5,))
            begin(u, (7,))
        else:
            arrive(u, (4, 6, 7))

    def position(j):
        for d in range(1, 8):
            swap_in(j, d).wait_recv()
        high, low = halves(got[j])
        placed = nn(spread[...], high) + nn(spread[...], low)
        placed = placed.T
        for l in range(2):
            for p in range(16):
                at = l * 128 + p * 8
                rhs[j, z // 2, z % 2, y // 2, y % 2, l, :, p * 128 : p * 128 + 128] = placed[
                    at : at + 8, :
                ]

    def chip(t):
        return (x + 2 + 3 * t - t * (t - 1) // 2) % 4

    def split_bem(i):
        bem_load(i).wait()

        @pl.loop(0, 16)
        def _(k):
            src = pl.ds(pl.multiple_of(k * 16, 16), 16)
            dst = pl.ds(pl.multiple_of(i * 256 + k * 16, 16), 16)
            for t in range(4):
                cols = pl.ds(pl.multiple_of(chip(t) * 256, 256), 256)
                real, imag = stage[i % 2, 0, src, cols], stage[i % 2, 1, src, cols]
                for m, value in enumerate((real, imag - real, real + imag)):
                    high, low = halves(value)
                    bem_hi[m, dst, t * 256 : t * 256 + 256] = high
                    bem_lo[m, dst, t * 256 : t * 256 + 256] = low

        if i + 2 < 8:
            bem_load(i + 2).start()

    def split_rhs(j):
        for c in range(0, 16, 2):
            at = (j, c // 8, (c // 4) % 2, (c // 2) % 2)
            real = rhs[at + (slice(None), 0)].reshape(16, 2048)
            imag = rhs[at + (slice(None), 1)].reshape(16, 2048)
            for m, value in enumerate((real + imag, real, imag)):
                high, low = halves(value)
                rhs_hi[m, c * 8 : c * 8 + 16, :] = high
                rhs_lo[m, c * 8 : c * 8 + 16, :] = low

    def pair(j, t):
        return pltpu.make_async_remote_copy(
            theirs.at[j, t], joined.at[j, t], pair_s.at[j, t], pair_r.at[j, t],
            device_id=(x * 2 + 1 - core, col), device_id_type=MESH,
        )

    def share(j, t):
        return pltpu.make_async_remote_copy(
            mine.at[j, t], partial.at[j, t], sum_s.at[j, t], sum_r.at[j, t],
            device_id=(chip(t) * 2 + core, col), device_id_type=MESH,
        )

    def multiply(j, t):
        cols = pl.ds(pl.multiple_of(t * 256, 256), 256)
        both, cross, twin = [
            nn(rhs_hi[m], bem_hi[m, :, cols])
            + nn(rhs_hi[m], bem_lo[m, :, cols])
            + nn(rhs_lo[m], bem_hi[m, :, cols])
            for m in range(3)
        ]
        for l, value in enumerate((both - twin, both + cross)):
            left, right = value[:, :128], value[:, 128:]
            mine[j, t, l] = jnp.where(core == 0, left, right)
            theirs[j, t, l] = jnp.where(core == 0, right, left)
        pair(j, t).start()

    def pass_on(j, t):
        pair(j, t).wait_recv()
        mine[j, t] = mine[j, t] + joined[j, t]

        if t < 3:
            share(j, t).start()

    def finish(j):
        for t in range(3):
            share(j, t).wait_recv()
        eight = pl.ds(j * 8, 8)
        for l in range(2):
            value = mine[j, 3, l] + partial[j, 0, l] + partial[j, 1, l] + partial[j, 2, l]
            value = value.reshape(16, 8, 128)
            field_ref[l, :, eight, :] = value
            grad[...] += jnp.sum(fwd[l, :, eight, :] * value, axis=0)

    def weigh():
        loads[2].wait()
        weight = jnp.broadcast_to(weight_ref[...], (128, 512)).T.reshape(16, 32, 128)
        for l in range(2):
            fwd[l] = fwd[l] * weight

    def act(op):
        what = op[0]
        if what == "V":
            gather_stage(op[2], op[1])
        elif what == "T":
            tractions(op[1])
        elif what == "X":
            exchange(op[1])
        elif what == "R":
            pass_on(op[1], op[2])
        elif what == "F":
            finish(op[1])
        elif what == "P":
            position(op[1])
        else:
            split_bem(op[1])

    mask_map()
    tractions(0)
    pl.semaphore_wait(barrier, 11)
    exchange(0)
    build_spread()
    for op in OPENING:
        act(op)
    weigh()

    for g, (j, low, high) in enumerate(GROUPS):
        for op in EVENTS.get((g, low), ()):
            act(op)
        split_rhs(j)

        @pl.loop(low, high)
        def _(t):
            for k in range(low + 1, high):
                if (g, k) in EVENTS:

                    @pl.when(t == k)
                    def _():
                        for op in EVENTS[(g, k)]:
                            act(op)

            multiply(j, t)
            for k in range(low, high):
                if (g, k) in AFTER:

                    @pl.when(t == k)
                    def _():
                        for op in AFTER[(g, k)]:
                            act(op)

    grad_ref[...] = jnp.sum(grad[...], axis=0, keepdims=True)

    for u in range(len(UNITS)):
        for f in range(2):
            for kind in range(8):
                for step in steps(kind):
                    hop(u, f, kind, step)[0]().wait_send()
    for j in range(CHUNKS):
        for d in range(1, 8):
            swap(j, d).wait_send()
        for t in range(4):
            pair(j, t).wait_send()
        for t in range(3):
            share(j, t).wait_send()


def on_device(
    bem, face_disp, face_map, dof_count, elem_target, live_count, forward_field, power_weight
):
    vmem = pl.BlockSpec(memory_space=pltpu.VMEM)
    hbm = pl.BlockSpec(memory_space=pl.ANY)
    dma = pltpu.SemaphoreType.DMA
    field, gradient = pl.pallas_call(
        kernel,
        out_shape=(pltpu.VMEM((2, 16, 32, 128), F32), pltpu.VMEM((1, 128), F32)),
        in_specs=[pl.BlockSpec(memory_space=pltpu.SMEM), vmem, vmem, vmem, hbm, hbm, hbm, hbm],
        out_specs=(vmem, vmem),
        scratch_shapes=[
            pltpu.VMEM((2, 25, 32, 256), F32),
            pltpu.VMEM((25, 16, 256), F32),
            pltpu.VMEM((2, 16, 32, 128), F32),
            pltpu.VMEM((2, 2, 256, 1024), F32),
            pltpu.VMEM((256, 256), BF16),
            pltpu.VMEM((128, 256), BF16),
            pltpu.VMEM((256, 256), F32),
            pltpu.VMEM((CHUNKS, 256, 256), F32),
            pltpu.VMEM((CHUNKS, 256, 256), F32),
            pltpu.VMEM((CHUNKS, 2, 2, 2, 2, 2, 8, 2048), F32),
            pltpu.VMEM((3, 128, 2048), BF16),
            pltpu.VMEM((3, 128, 2048), BF16),
            pltpu.VMEM((3, 2048, 1024), BF16),
            pltpu.VMEM((3, 2048, 1024), BF16),
            pltpu.VMEM((CHUNKS, 4, 2, 128, 128), F32),
            pltpu.VMEM((CHUNKS, 4, 2, 128, 128), F32),
            pltpu.VMEM((CHUNKS, 4, 2, 128, 128), F32),
            pltpu.VMEM((CHUNKS, 3, 2, 128, 128), F32),
            pltpu.VMEM((8, 128), F32),
            dma((3,)),
            dma((2,)),
            dma((CHUNKS, 7)),
            dma((CHUNKS, 7)),
            dma((len(UNITS), 2, 12)),
            dma((len(UNITS), 2, 12)),
            dma((CHUNKS, 4)),
            dma((CHUNKS, 4)),
            dma((CHUNKS, 3)),
            dma((CHUNKS, 3)),
        ],
        compiler_params=pltpu.CompilerParams(
            collective_id=0, has_side_effects=True, vmem_limit_bytes=60 * 2**20
        ),
        cost_estimate=pl.CostEstimate(
            flops=26 * 10**9, bytes_accessed=20 * 10**6, transcendentals=0
        ),
        name="adjoint",
    )(
        live_count,
        elem_target.reshape(1, 2048),
        dof_count.reshape(1, 256),
        power_weight.reshape(1, 512),
        bem,
        face_disp,
        jnp.transpose(face_map, (1, 0, 2)),
        forward_field.reshape(2, 16, 32, 128),
    )
    return field.reshape(2, 512, 128), gradient.reshape(128)


def solution(mesh):
    placed = (
        P(None, "row", "col"),
        P(None, None, "col", "row"),
        P(None, None, "row"),
        P("row"),
        P(),
        P(),
        P(None, None, ("col", "row")),
        P(),
    )
    return jax.shard_map(
        on_device,
        mesh=mesh,
        in_specs=placed,
        out_specs=(P(None, None, ("col", "row")), P(("col", "row"))),
        check_vma=False,
    )
```

```python
import functools

import jax
import jax.numpy as jnp
from jax import lax
from jax.experimental import pallas as pl
from jax.experimental.pallas import tpu as pltpu
from jax.sharding import PartitionSpec as P

MESH = pl.DeviceIdType.MESH
F32 = jnp.float32
BF16 = jnp.bfloat16

CHUNKS = 4
UNITS = tuple((j, 0, 2048) for j in range(CHUNKS))
GROUPS = ((0, 0, 4), (1, 0, 4), (2, 0, 3), (3, 0, 4), (2, 3, 4))
OPENING = (
    ("T", 1), ("X", 1), ("P", 0), ("V", 0, 0), ("T", 2), ("X", 2), ("P", 1), ("V", 0, 1), ("B", 0),
    ("V", 1, 0), ("B", 1), ("B", 2), ("T", 3), ("X", 3), ("G", 0), ("V", 2, 0), ("B", 3), ("V", 1, 1),
    ("P", 2), ("B", 4), ("B", 5), ("V", 3, 0), ("V", 0, 2), ("B", 6), ("P", 3), ("V", 2, 1),
    ("B", 7), ("V", 4, 0),
)
EVENTS = {
    (0, 1): (
        ("V", 1, 2),
    ),
    (0, 2): (
        ("V", 3, 1), ("R", 0, 0),
    ),
    (0, 3): (
        ("V", 0, 3), ("R", 0, 1),
    ),
    (1, 0): (
        ("V", 2, 2), ("R", 0, 2), ("V", 4, 1),
    ),
    (1, 1): (
        ("V", 1, 3),
    ),
    (1, 3): (
        ("V", 3, 2), ("F", 0),
    ),
    (2, 0): (
        ("V", 2, 3), ("R", 1, 2), ("V", 4, 2),
    ),
    (2, 1): (
        ("V", 3, 3),
    ),
    (3, 0): (
        ("V", 4, 3), ("R", 2, 1), ("F", 1),
    ),
    (3, 3): (
        ("R", 3, 2),
    ),
}
AFTER = {
    (1, 0): (
        ("R", 0, 3),
    ),
    (1, 1): (
        ("R", 1, 0),
    ),
    (1, 2): (
        ("R", 1, 1),
    ),
    (2, 0): (
        ("R", 1, 3),
    ),
    (2, 1): (
        ("R", 2, 0),
    ),
    (3, 0): (
        ("R", 2, 2),
    ),
    (3, 1): (
        ("R", 3, 0),
    ),
    (3, 2): (
        ("R", 3, 1),
    ),
    (4, 3): (
        ("W", 0),
        ("R", 3, 3), ("R", 2, 3), ("F", 2), ("F", 3),
    ),
}
FORWARD = (2, 4, 6, 7)
SEM = (0, 2, 4, 5, 7, 8, 10, 11)

def nt(a, b):
    return lax.dot_general(a, b, (((1,), (1,)), ((), ())), preferred_element_type=F32)


def nn(a, b):
    return jnp.dot(a, b, preferred_element_type=F32)


def halves(value):
    high = value.astype(BF16)
    return high, (value - high.astype(F32)).astype(BF16)


def one_hot(condition):
    return jnp.where(condition, 1.0, 0.0).astype(BF16)


def kernel(
    live_ref, target_ref, dof_ref, weight_ref, bem_ref, disp_ref, map_ref, fwd_ref,
    field_ref, grad_ref,
    disp, fmap, fwd, stage, pick, spread, trac, comp, got, rhs, rhs_hi, rhs_lo, bem_hi, bem_lo,
    mine, theirs, joined, partial, grad,
    in_sem, bem_sem, swap_s, swap_r, ag_s, ag_r, pair_s, pair_r, sum_s, sum_r,
):
    row = lax.axis_index("row")
    col = lax.axis_index("col")
    x, core = row // 2, row % 2
    z, y = col // 4, col % 4

    barrier = pltpu.get_barrier_semaphore()
    for d in range(1, 8):
        pl.semaphore_signal(barrier, inc=1, device_id=((row + d) % 8, col), device_id_type=MESH)
    for d in (1, 3):
        near = ((z + d) % 4) * 4 + y
        pl.semaphore_signal(barrier, inc=1, device_id=(row, near), device_id_type=MESH)
        near = z * 4 + (y + d) % 4
        pl.semaphore_signal(barrier, inc=1, device_id=(row, near), device_id_type=MESH)

    loads = [
        pltpu.make_async_copy(map_ref, fmap, in_sem.at[0]),
        pltpu.make_async_copy(disp_ref, disp, in_sem.at[1]),
        pltpu.make_async_copy(fwd_ref, fwd, in_sem.at[2]),
    ]

    def bem_load(i):
        rows = pl.ds(pl.multiple_of(i * 256, 256), 256)
        return pltpu.make_async_copy(
            bem_ref.at[:, rows, :], stage.at[i % 2], bem_sem.at[i % 2]
        )

    loads[0].start()
    loads[1].start()
    bem_load(0).start()
    bem_load(1).start()
    loads[2].start()

    lane = lax.broadcasted_iota(jnp.int32, (8, 256), 1)
    line = lax.broadcasted_iota(jnp.int32, (8, 256), 0)
    count = jnp.zeros((8, 256), jnp.int32)
    for o in range(8):
        count = jnp.where(line == o, live_ref[o], count)
    live = lane < count
    target = jnp.concatenate([target_ref[:, o * 256 : o * 256 + 256] for o in range(8)], axis=0)
    block = target >> 7
    within = target & 127
    members = jnp.concatenate(
        [jnp.where(live & (block == b), 1.0, 0.0) for b in range(8)], axis=0
    )
    before = lax.broadcasted_iota(jnp.int32, (256, 256), 0) < lax.broadcasted_iota(
        jnp.int32, (256, 256), 1
    )
    ranks = members * nn(members.astype(BF16), one_hot(before))
    rank = ranks[0:8]
    for b in range(1, 8):
        rank = rank + ranks[b * 8 : b * 8 + 8]
    place = jnp.where(live, block * 32 + rank.astype(jnp.int32), -1)
    own = jnp.sum(jnp.where(line == row, place, 0), axis=0, keepdims=True)
    tall = lax.broadcasted_iota(jnp.int32, (256, 256), 0)
    pick[...] = one_hot(tall == own)
    grad[...] = jnp.zeros_like(grad)

    def build_spread():
        wide = lax.broadcasted_iota(jnp.int32, (128, 256), 0)
        here = jnp.where(live & (block == row), place - row * 32 + line * 32, -1)
        total = jnp.zeros((128, 256), F32)
        for o in range(8):
            total = total + nt(
                one_hot(wide == within[o : o + 1]), one_hot(tall == here[o : o + 1])
            )
        spread[...] = total.astype(BF16)

    def mask_map():
        loads[0].wait()
        node = lax.broadcasted_iota(jnp.int32, (25, 16, 256), 0)
        used = node < dof_ref[...].reshape(1, 1, 256)
        fmap[...] = jnp.where(used, fmap[...], 0.0)
        loads[1].wait()

    def swap(j, d):
        to = (row + d) % 8
        return pltpu.make_async_remote_copy(
            comp.at[j, pl.ds(pl.multiple_of(to * 32, 32), 32), :],
            got.at[j, pl.ds(pl.multiple_of(row * 32, 32), 32), :],
            swap_s.at[j, d - 1], swap_r.at[j, d - 1],
            device_id=(to, col), device_id_type=MESH,
        )

    def swap_in(j, d):
        origin = (row + 8 - d) % 8
        return pltpu.make_async_remote_copy(
            comp.at[j, pl.ds(pl.multiple_of(row * 32, 32), 32), :],
            got.at[j, pl.ds(pl.multiple_of(origin * 32, 32), 32), :],
            swap_s.at[j, d - 1], swap_r.at[j, d - 1],
            device_id=((row + d) % 8, col), device_id_type=MESH,
        )

    def tractions(j):
        eight = pl.ds(j * 8, 8)
        for group in range(4):
            sums = [[None] * 4, [None] * 4]
            for q in range(25):
                value = [disp[l, q, eight, :] for l in range(2)]
                for k in range(4):
                    at = group * 4 + k
                    scale = fmap[q, at : at + 1, :]
                    for l in range(2):
                        term = scale * value[l]
                        sums[l][k] = term if q == 0 else sums[l][k] + term
            for l in range(2):
                for k in range(4):
                    at = l * 128 + (group * 4 + k) * 8
                    trac[at : at + 8, :] = sums[l][k]
        high, low = halves(trac[...])
        comp[j] = nt(pick[...], high) + nt(pick[...], low)

    def exchange(j):
        for d in (4, 5, 2, 3, 6, 7, 1):
            swap(j, d).start()
        rows = pl.ds(pl.multiple_of(row * 32, 32), 32)
        got[j, rows, :] = comp[j, rows, :]

    def slots(f, first, second):
        def sel(v):
            kind, a = v
            return (a // 2, a % 2) if kind == "one" else (slice(None), a)

        fi, se = sel(first), sel(second)
        return fi + se if f == 0 else se + fi

    def part(ref, u, f, first, second):
        j, lane0, size = UNITS[u]
        return ref.at[(j,) + slots(f, first, second) + (f, slice(None), pl.ds(lane0, size))]

    def ring(f):
        return (z, y) if f == 0 else (y, z)

    def away(f, axis, step):
        v1, v2 = ring(f)
        if axis == 0:
            v1 = (v1 + step + 4) % 4
        else:
            v2 = (v2 + step + 4) % 4
        return (row, v1 * 4 + v2) if f == 0 else (row, v2 * 4 + v1)

    turn = 1 - 2 * core

    def hop(u, f, kind, step):
        v1, v2 = ring(f)
        back = lambda v, n: (v + 4 - n * step) % 4
        one = lambda v: ("one", v)
        par = ("par", (v1 + 1) % 2)
        far = one((v1 + 2) % 4)
        axis, out, into = {
            0: (0, (one(v1), one(v2)), (one(back(v1, 1)), one(v2))),
            1: (1, (one(v1), one(v2)), (one(v1), one(back(v2, 1)))),
            2: (0, (one(back(v1, 1)), one(v2)), (far, one(v2))),
            3: (1, (par, one(v2)), (par, one(back(v2, 1)))),
            4: (1, (one(v1), one(back(v2, 1))), (one(v1), one((v2 + 2) % 4))),
            5: (1, (far, one(v2)), (far, one(back(v2, 1)))),
            6: (1, (par, one(back(v2, 1))), (par, one((v2 + 2) % 4))),
            7: (1, (far, one(back(v2, 1))), (far, one((v2 + 2) % 4))),
        }[kind]
        n = SEM[kind] + (0 if kind in FORWARD or step == 1 else 1)
        make = lambda src, dst: pltpu.make_async_remote_copy(
            part(rhs, u, f, *src), part(rhs, u, f, *dst),
            ag_s.at[u, f, n], ag_r.at[u, f, n],
            device_id=away(f, axis, step), device_id_type=MESH,
        )
        return lambda: make(out, out), lambda: make(out, into)

    def steps(kind):
        return (turn,) if kind in FORWARD else (1, -1)

    def begin(u, kinds):
        for kind in kinds:
            for f in range(2):
                for step in steps(kind):
                    hop(u, f, kind, step)[0]().start()

    def arrive(u, kinds):
        for kind in kinds:
            for f in range(2):
                for step in steps(kind):
                    hop(u, f, kind, step)[1]().wait_recv()

    def gather_stage(u, which):
        if which == 0:
            begin(u, (0, 1))
        elif which == 1:
            arrive(u, (0,))
            begin(u, (2, 3))
            arrive(u, (1,))
            begin(u, (4,))
        elif which == 2:
            arrive(u, (2,))
            begin(u, (5,))
            arrive(u, (3,))
            begin(u, (6,))
        elif which == 3:
            arrive(u, (5,))
            begin(u, (7,))
        else:
            arrive(u, (4, 6, 7))

    def position(j):
        for d in range(1, 8):
            swap_in(j, d).wait_recv()
        high, low = halves(got[j])
        placed = nn(spread[...], high) + nn(spread[...], low)
        placed = placed.T
        for l in range(2):
            for p in range(16):
                at = l * 128 + p * 8
                rhs[j, z // 2, z % 2, y // 2, y % 2, l, :, p * 128 : p * 128 + 128] = placed[
                    at : at + 8, :
                ]

    def chip(t):
        return (x + 2 + 3 * t - t * (t - 1) // 2) % 4

    def split_bem(i):
        bem_load(i).wait()

        @pl.loop(0, 16)
        def _(k):
            src = pl.ds(pl.multiple_of(k * 16, 16), 16)
            dst = pl.ds(pl.multiple_of(i * 256 + k * 16, 16), 16)
            for t in range(4):
                cols = pl.ds(pl.multiple_of(chip(t) * 256, 256), 256)
                real, imag = stage[i % 2, 0, src, cols], stage[i % 2, 1, src, cols]
                for m, value in enumerate((real, imag - real, real + imag)):
                    high, low = halves(value)
                    bem_hi[m, dst, t * 256 : t * 256 + 256] = high
                    bem_lo[m, dst, t * 256 : t * 256 + 256] = low

        if i + 2 < 8:
            bem_load(i + 2).start()

    def split_rhs(j):
        for c in range(0, 16, 2):
            at = (j, c // 8, (c // 4) % 2, (c // 2) % 2)
            real = rhs[at + (slice(None), 0)].reshape(16, 2048)
            imag = rhs[at + (slice(None), 1)].reshape(16, 2048)
            for m, value in enumerate((real + imag, real, imag)):
                high, low = halves(value)
                rhs_hi[m, c * 8 : c * 8 + 16, :] = high
                rhs_lo[m, c * 8 : c * 8 + 16, :] = low

    def pair(j, t):
        return pltpu.make_async_remote_copy(
            theirs.at[j, t], joined.at[j, t], pair_s.at[j, t], pair_r.at[j, t],
            device_id=(x * 2 + 1 - core, col), device_id_type=MESH,
        )

    def share(j, t):
        return pltpu.make_async_remote_copy(
            mine.at[j, t], partial.at[j, t], sum_s.at[j, t], sum_r.at[j, t],
            device_id=(chip(t) * 2 + core, col), device_id_type=MESH,
        )

    def multiply(j, t):
        cols = pl.ds(pl.multiple_of(t * 256, 256), 256)
        both, cross, twin = [
            nn(rhs_hi[m], bem_hi[m, :, cols])
            + nn(rhs_hi[m], bem_lo[m, :, cols])
            + nn(rhs_lo[m], bem_hi[m, :, cols])
            for m in range(3)
        ]
        for l, value in enumerate((both - twin, both + cross)):
            left, right = value[:, :128], value[:, 128:]
            mine[j, t, l] = jnp.where(core == 0, left, right)
            theirs[j, t, l] = jnp.where(core == 0, right, left)
        pair(j, t).start()

    def pass_on(j, t):
        pair(j, t).wait_recv()
        mine[j, t] = mine[j, t] + joined[j, t]

        if t < 3:
            share(j, t).start()

    def finish(j):
        for t in range(3):
            share(j, t).wait_recv()
        eight = pl.ds(j * 8, 8)
        for l in range(2):
            value = mine[j, 3, l] + partial[j, 0, l] + partial[j, 1, l] + partial[j, 2, l]
            value = value.reshape(16, 8, 128)
            field_ref[l, :, eight, :] = value
            grad[...] += jnp.sum(fwd[l, :, eight, :] * value, axis=0)

    def weigh():
        loads[2].wait()
        weight = jnp.broadcast_to(weight_ref[...], (128, 512)).T.reshape(16, 32, 128)
        for l in range(2):
            fwd[l] = fwd[l] * weight

    def drain():
        for u in range(len(UNITS)):
            for f in range(2):
                for kind in range(8):
                    for step in steps(kind):
                        hop(u, f, kind, step)[0]().wait_send()
        for j in range(CHUNKS):
            for d in range(1, 8):
                swap(j, d).wait_send()

    def act(op):
        what = op[0]
        if what == "V":
            gather_stage(op[2], op[1])
        elif what == "T":
            tractions(op[1])
        elif what == "X":
            exchange(op[1])
        elif what == "G":
            weigh()
        elif what == "W":
            drain()
        elif what == "R":
            pass_on(op[1], op[2])
        elif what == "F":
            finish(op[1])
        elif what == "P":
            position(op[1])
        else:
            split_bem(op[1])

    mask_map()
    tractions(0)
    pl.semaphore_wait(barrier, 11)
    exchange(0)
    build_spread()
    for op in OPENING:
        act(op)

    for g, (j, low, high) in enumerate(GROUPS):
        for op in EVENTS.get((g, low), ()):
            act(op)
        split_rhs(j)

        @pl.loop(low, high)
        def _(t):
            for k in range(low + 1, high):
                if (g, k) in EVENTS:

                    @pl.when(t == k)
                    def _():
                        for op in EVENTS[(g, k)]:
                            act(op)

            multiply(j, t)
            for k in range(low, high):
                if (g, k) in AFTER:

                    @pl.when(t == k)
                    def _():
                        for op in AFTER[(g, k)]:
                            act(op)

    grad_ref[...] = jnp.sum(grad[...], axis=0, keepdims=True)

    for j in range(CHUNKS):
        for t in range(4):
            pair(j, t).wait_send()
        for t in range(3):
            share(j, t).wait_send()


def on_device(
    bem, face_disp, face_map, dof_count, elem_target, live_count, forward_field, power_weight
):
    vmem = pl.BlockSpec(memory_space=pltpu.VMEM)
    hbm = pl.BlockSpec(memory_space=pl.ANY)
    dma = pltpu.SemaphoreType.DMA
    field, gradient = pl.pallas_call(
        kernel,
        out_shape=(pltpu.VMEM((2, 16, 32, 128), F32), pltpu.VMEM((1, 128), F32)),
        in_specs=[pl.BlockSpec(memory_space=pltpu.SMEM), vmem, vmem, vmem, hbm, hbm, hbm, hbm],
        out_specs=(vmem, vmem),
        scratch_shapes=[
            pltpu.VMEM((2, 25, 32, 256), F32),
            pltpu.VMEM((25, 16, 256), F32),
            pltpu.VMEM((2, 16, 32, 128), F32),
            pltpu.VMEM((2, 2, 256, 1024), F32),
            pltpu.VMEM((256, 256), BF16),
            pltpu.VMEM((128, 256), BF16),
            pltpu.VMEM((256, 256), F32),
            pltpu.VMEM((CHUNKS, 256, 256), F32),
            pltpu.VMEM((CHUNKS, 256, 256), F32),
            pltpu.VMEM((CHUNKS, 2, 2, 2, 2, 2, 8, 2048), F32),
            pltpu.VMEM((3, 128, 2048), BF16),
            pltpu.VMEM((3, 128, 2048), BF16),
            pltpu.VMEM((3, 2048, 1024), BF16),
            pltpu.VMEM((3, 2048, 1024), BF16),
            pltpu.VMEM((CHUNKS, 4, 2, 128, 128), F32),
            pltpu.VMEM((CHUNKS, 4, 2, 128, 128), F32),
            pltpu.VMEM((CHUNKS, 4, 2, 128, 128), F32),
            pltpu.VMEM((CHUNKS, 3, 2, 128, 128), F32),
            pltpu.VMEM((8, 128), F32),
            dma((3,)),
            dma((2,)),
            dma((CHUNKS, 7)),
            dma((CHUNKS, 7)),
            dma((len(UNITS), 2, 12)),
            dma((len(UNITS), 2, 12)),
            dma((CHUNKS, 4)),
            dma((CHUNKS, 4)),
            dma((CHUNKS, 3)),
            dma((CHUNKS, 3)),
        ],
        compiler_params=pltpu.CompilerParams(
            collective_id=0, has_side_effects=True, vmem_limit_bytes=60 * 2**20
        ),
        cost_estimate=pl.CostEstimate(
            flops=26 * 10**9, bytes_accessed=20 * 10**6, transcendentals=0
        ),
        name="adjoint",
    )(
        live_count,
        elem_target.reshape(1, 2048),
        dof_count.reshape(1, 256),
        power_weight.reshape(1, 512),
        bem,
        face_disp,
        jnp.transpose(face_map, (1, 0, 2)),
        forward_field.reshape(2, 16, 32, 128),
    )
    return field.reshape(2, 512, 128), gradient.reshape(128)


def solution(mesh):
    placed = (
        P(None, "row", "col"),
        P(None, None, "col", "row"),
        P(None, None, "row"),
        P("row"),
        P(),
        P(),
        P(None, None, ("col", "row")),
        P(),
    )
    return jax.shard_map(
        on_device,
        mesh=mesh,
        in_specs=placed,
        out_specs=(P(None, None, ("col", "row")), P(("col", "row"))),
        check_vma=False,
    )
```
